256 devices in a mesh: dp: 64 (over z, y, core), tensor: 4 (over x).
Axes of the slice: x: 4, y: 4, z: 8, core: 2. Of those that a mesh axis runs over, the one named last changes fastest.
Arguments:
- query: bfloat16 [512, 8192], P('dp', 'tensor'), may hold values from -8 to 8
- incoming_key: bfloat16 [512, 1024], P('dp', 'tensor'), may hold values from -5 to 5
- incoming_value: bfloat16 [512, 1024], P('dp', 'tensor'), may hold values from -5 to 5
- cycle_key_cache: bfloat16 [512, 1024, 1024], P('dp', None, 'tensor'), may hold values from -8 to 8
- cycle_value_cache: bfloat16 [512, 1024, 1024], P('dp', None, 'tensor'), may hold values from -5 to 5
- position: int32 [512], P('dp'), may hold values from 1 to 2047
- tenant: int32 [512], replicated, may hold values from 0 to 511
- tenant_adapter_index: int32 [512], replicated, may hold values from 0 to 511, each once
- output_weight: bfloat16 [8192, 8192], P('tensor', 'dp'), may hold values from -0.5 to 0.5
- adapter_down_weight: bfloat16 [512, 8192, 64], P('dp', 'tensor'), may hold values from -0.5 to 0.5
- adapter_up_weight: bfloat16 [512, 64, 8192], P('dp', None, 'tensor'), may hold values from -0.75 to 0.75
Outputs:
- mixed: bfloat16 [512, 8192], P('dp', 'tensor')
The draws below stay inside these ranges and needn't reach their ends.
All inputs are finite; a program needn't handle non-finite values.
Results may differ from the reference program's by a relative error of at most 0.012.
Values may be sent and summed in bfloat16 or wider, within the bound.
No kernel may reach another device: no remote copies, remote signals or barrier semaphores. Data moves between devices by JAX's collectives and lax.ppermute only.
A program may use at most 64 MiB of HBM per device.

```python
import math
import jax
import jax.numpy as jnp
import numpy as np
from jax import lax

MODEL_WIDTH = 8192
QUERY_HEADS = 64
KVH = 8
HEAD_SIZE = 128
ADAPTER_RANK = 64
CACHE = 1024
SESSIONS = 512
ADAPTER_COUNT = 512


def draw_query(key, part):
    key = jax.random.fold_in(key, 1)
    values = jax.random.truncated_normal(key, -4.0, 4.0, (SESSIONS, QUERY_HEADS * HEAD_SIZE))
    return values.astype(jnp.bfloat16)


def draw_cycle_key_cache(key, part):
    key = jax.random.fold_in(key, 2)
    values = jax.random.truncated_normal(key, -4.0, 4.0, (SESSIONS, CACHE, KVH * HEAD_SIZE))
    return values.astype(jnp.bfloat16)


def plant(result, rng, low, largest):
    place = [jax.random.randint(jax.random.fold_in(rng, axis), (), 0, length) for axis, length in enumerate(result.shape)]
    longest = result.shape.index(max(result.shape))
    beside = place[:longest] + [(place[longest] + 1) % result.shape[longest]] + place[longest + 1:]
    return result.at[tuple(place)].set(low).at[tuple(beside)].set(largest)


def level_of(rng, dims, split, least, largest):
    loudness, own = 1.0, jax.random.fold_in(rng, 6)
    for dim, shards_of in split:
        draws = jnp.exp(jax.random.uniform(jax.random.fold_in(own, dim), (shards_of,), jnp.float32, least / len(split), largest / len(split)))
        loudness = loudness * jnp.repeat(draws, dims[dim] // shards_of).reshape([-1 if axis == dim else 1 for axis in range(len(dims))])
    return loudness


def cumulative_ranks(count, lean):
    portions = [(1 << 20) // math.isqrt(standing ** lean) + 1 for standing in range(1, count + 1)]
    scale = 1 + sum(portions) // (1 << 30)
    return np.cumsum(np.array([max(1, weight // scale) for weight in portions]))


def ranked_ids(own_key, dims, number_of, lean):
    grid = cumulative_ranks(number_of, lean)
    ticket = jax.random.randint(jax.random.fold_in(own_key, 1), dims, 0, int(grid[number_of - 1]))
    standing = jnp.searchsorted(jnp.asarray(grid, jnp.int32), ticket, side="right")
    return jax.random.permutation(jax.random.fold_in(own_key, 2), number_of)[standing].astype(jnp.int32)


def scatter_about(own_key, shape, scale, reach, cuts=(), held_as=jnp.bfloat16):
    factor_of = level_of(own_key, shape, cuts, -0.22, 0.18) if cuts else 1.0
    result = jax.random.normal(own_key, shape, jnp.float32) * scale * factor_of
    return jnp.minimum(jnp.maximum(result, -reach), reach).astype(held_as)


def setup_inputs(seed: int = 0) -> dict:
    seeds = jax.random.split(jax.random.key(seed), 12)
    query = draw_query(jax.random.fold_in(seeds[11], 71), 0)
    incoming_key = scatter_about(seeds[1], (SESSIONS, KVH * HEAD_SIZE), 1.0, 5.0, ((0, 64), (1, 4)))
    incoming_value = scatter_about(seeds[2], (SESSIONS, KVH * HEAD_SIZE), 1.0, 5.0, ((0, 64), (1, 4)))
    cycle_key_cache = draw_cycle_key_cache(jax.random.fold_in(seeds[11], 71), 0)
    cycle_value_cache = scatter_about(seeds[4], (SESSIONS, CACHE, KVH * HEAD_SIZE), 1.0, 5.0, ((0, 64), (2, 4)))
    position = plant(jax.random.randint(seeds[5], (SESSIONS,), 1, 2 * CACHE), jax.random.fold_in(seeds[5], 1), 1, (2 * CACHE) - 1).astype(jnp.int32)
    tenant = plant(ranked_ids(seeds[6], (SESSIONS,), ADAPTER_COUNT, 2), jax.random.fold_in(seeds[6], 3), 0, ADAPTER_COUNT - 1).astype(jnp.int32)
    tenant_adapter_index = jax.random.permutation(seeds[7], ADAPTER_COUNT).astype(jnp.int32)
    output_weight = scatter_about(seeds[8], (QUERY_HEADS * HEAD_SIZE, MODEL_WIDTH), HEAD_SIZE ** -0.5, 0.5, ((0, 4), (1, 64)))
    adapter_down_weight = scatter_about(seeds[9], (ADAPTER_COUNT, QUERY_HEADS * HEAD_SIZE, ADAPTER_RANK), HEAD_SIZE ** -0.5, 0.5, ((0, 64), (1, 4)))
    adapter_up_weight = scatter_about(seeds[10], (ADAPTER_COUNT, ADAPTER_RANK, MODEL_WIDTH), ADAPTER_RANK ** -0.5, 0.75, ((0, 64), (2, 4)))
    return dict(query=query, incoming_key=incoming_key, incoming_value=incoming_value, cycle_key_cache=cycle_key_cache, cycle_value_cache=cycle_value_cache, position=position, tenant=tenant, tenant_adapter_index=tenant_adapter_index, output_weight=output_weight, adapter_down_weight=adapter_down_weight, adapter_up_weight=adapter_up_weight)


adapter_scale = 0.5


def attend_one(args):
    query_row, key_row, value_row, key_rows, value_rows, seen = args
    slots = jnp.arange(CACHE, dtype=jnp.int32)
    here = slots == (seen % CACHE)
    live = (slots < seen) & jnp.logical_not(here)
    inverse = HEAD_SIZE ** -0.5
    group = QUERY_HEADS // KVH
    query3 = query_row.astype(jnp.float32).reshape(KVH, group, HEAD_SIZE)
    keys3 = key_rows.astype(jnp.float32).reshape(CACHE, KVH, HEAD_SIZE)
    values3 = value_rows.astype(jnp.float32).reshape(CACHE, KVH, HEAD_SIZE)
    scores = jnp.einsum('kgd,ckd->kgc', query3, keys3) * inverse
    fresh = jnp.einsum('kgd,kd->kg', query3, key_row.astype(jnp.float32).reshape(KVH, HEAD_SIZE)) * inverse
    scores = jnp.where(live[None, None, :], scores, jnp.float32(-1e30))
    top = jnp.maximum(jnp.max(scores, axis=-1), fresh)
    weights = jnp.exp(scores - top[..., None])
    fresh_weight = jnp.exp(fresh - top)
    total = jnp.sum(weights, axis=-1) + fresh_weight
    probs = (weights / total[..., None]).astype(jnp.bfloat16)
    fresh_prob = (fresh_weight / total).astype(jnp.bfloat16)
    attended = jnp.einsum('kgc,ckd->kgd', probs.astype(jnp.float32), values3)
    attended = attended + fresh_prob.astype(jnp.float32)[..., None] * value_row.astype(jnp.float32).reshape(KVH, 1, HEAD_SIZE)
    return attended.reshape(QUERY_HEADS * HEAD_SIZE).astype(jnp.bfloat16)


def reference(query, incoming_key, incoming_value, cycle_key_cache, cycle_value_cache, position, tenant, tenant_adapter_index, output_weight, adapter_down_weight, adapter_up_weight):
    attended = lax.map(attend_one, (query, incoming_key, incoming_value, cycle_key_cache, cycle_value_cache, position))
    base_output = jnp.dot(attended, output_weight, preferred_element_type=jnp.float32)
    slot_of = tenant_adapter_index[tenant].astype(jnp.int32)

    def adapt(args):
        row, cycle_position = args
        down_weight = lax.dynamic_index_in_dim(adapter_down_weight, cycle_position, 0, keepdims=False)
        up_weight = lax.dynamic_index_in_dim(adapter_up_weight, cycle_position, 0, keepdims=False)
        rank = jnp.dot(row, down_weight, preferred_element_type=jnp.float32).astype(jnp.bfloat16)
        return jnp.dot(rank, up_weight, preferred_element_type=jnp.float32).astype(jnp.bfloat16)

    adapter_delta = lax.map(adapt, (attended, slot_of))
    return (base_output + adapter_scale * adapter_delta.astype(jnp.float32)).astype(jnp.bfloat16)
```

```python
import jax
import jax.numpy as jnp
import numpy as np
from jax import lax
from jax.sharding import Mesh, PartitionSpec as P

HEAD_SIZE = 128
adapter_scale = 0.5
NZ, NY, NC, NX = 8, 4, 2, 4
DP = ("z", "y", "c")


def attend(query, incoming_key, incoming_value, cycle_key_cache, cycle_value_cache, position):
    sessions = query.shape[0]
    cache_len = cycle_key_cache.shape[1]
    heads_kv = cycle_key_cache.shape[2] // HEAD_SIZE
    group = query.shape[1] // (heads_kv * HEAD_SIZE)
    inverse = HEAD_SIZE ** (-0.5)
    slots = jnp.arange(cache_len, dtype=jnp.int32)
    here = slots[None, :] == (position % cache_len)[:, None]
    live = (slots[None, :] < position[:, None]) & jnp.logical_not(here)
    query4 = query.reshape(sessions, heads_kv, group, HEAD_SIZE)
    keys4 = cycle_key_cache.reshape(sessions, cache_len, heads_kv, HEAD_SIZE)
    values4 = cycle_value_cache.reshape(sessions, cache_len, heads_kv, HEAD_SIZE)
    scores = (
        jnp.einsum("skgd,sckd->skgc", query4, keys4, preferred_element_type=jnp.float32) * inverse
    )
    fresh = (
        jnp.einsum(
            "skgd,skd->skg",
            query4,
            incoming_key.reshape(sessions, heads_kv, HEAD_SIZE),
            preferred_element_type=jnp.float32,
        )
        * inverse
    )
    scores = jnp.where(live[:, None, None, :], scores, jnp.float32(-1e30))
    top = jnp.maximum(jnp.max(scores, axis=-1), fresh)
    weights = jnp.exp(scores - top[..., None])
    fresh_weight = jnp.exp(fresh - top)
    total = jnp.sum(weights, axis=-1) + fresh_weight
    probs = (weights / total[..., None]).astype(jnp.bfloat16)
    fresh_prob = (fresh_weight / total).astype(jnp.bfloat16)
    attended = jnp.einsum("skgc,sckd->skgd", probs, values4, preferred_element_type=jnp.float32)
    attended = attended + fresh_prob.astype(jnp.float32)[..., None] * incoming_value.reshape(
        sessions, heads_kv, 1, HEAD_SIZE
    ).astype(jnp.float32)
    return attended.reshape(sessions, heads_kv * group * HEAD_SIZE).astype(jnp.bfloat16)


def swap_cores(x):
    return lax.ppermute(x, "c", [(0, 1), (1, 0)])


def local(
    query,
    incoming_key,
    incoming_value,
    cycle_key_cache,
    cycle_value_cache,
    position,
    tenant,
    tenant_adapter_index,
    output_weight,
    adapter_down_weight,
    adapter_up_weight,
):
    bf16, f32 = jnp.bfloat16, jnp.float32
    kept = adapter_down_weight.shape[0]
    rank = adapter_down_weight.shape[2]
    features = adapter_down_weight.shape[1]
    cols = output_weight.shape[1]
    quarter = adapter_up_weight.shape[2]
    mine_n = query.shape[0]
    half = NY * NZ * mine_n
    core = lax.axis_index("c")
    home = lax.axis_index(DP)
    x_here = lax.axis_index("x")

    attended = attend(
        query, incoming_key, incoming_value, cycle_key_cache, cycle_value_cache, position
    )

    along_z = lax.all_to_all(
        jnp.broadcast_to(attended[None], (NZ,) + attended.shape), "z", 0, 0, tiled=True
    ).reshape(NZ * mine_n, features)
    own = lax.all_to_all(
        jnp.broadcast_to(along_z[None], (NY,) + along_z.shape), "y", 0, 0, tiled=True
    ).reshape(half, features)
    other = swap_cores(own)

    tenants_all = tenant_adapter_index.shape[0]
    matches = tenant[:, None] == jnp.arange(tenants_all, dtype=jnp.int32)[None, :]
    slot_of = jnp.sum(jnp.where(matches, tenant_adapter_index[None, :], 0), axis=1)
    slot_by_core = slot_of.reshape(NZ, NY, NC, mine_n).transpose(2, 1, 0, 3).reshape(NC, half)
    slot_own = jnp.where(core == 0, slot_by_core[0], slot_by_core[1])
    slot_other = jnp.where(core == 0, slot_by_core[1], slot_by_core[0])
    my_slots = home * kept + jnp.arange(kept, dtype=jnp.int32)

    down = adapter_down_weight

    def rank_terms(rows, slots):
        portion = jnp.einsum("mj,hju->hum", rows, down, preferred_element_type=f32)
        mine = slots[None, :] == my_slots[:, None]
        return jnp.sum(jnp.where(mine[:, None, :], portion, 0.0), axis=0)

    rank_part = jnp.concatenate(
        [rank_terms(own, slot_own), rank_terms(other, slot_other)], axis=1
    ).astype(bf16)
    base_part = jnp.concatenate(
        [
            jnp.dot(own, output_weight, preferred_element_type=f32),
            jnp.dot(other, output_weight, preferred_element_type=f32),
        ],
        axis=0,
    ).astype(bf16)

    rank_full = rank_part.astype(f32)
    for shift in (2, 1, 3):
        got = lax.ppermute(rank_part, "x", [(i, (i + shift) % NX) for i in range(NX)])
        rank_full = rank_full + got.astype(f32)
    rank_full = rank_full.astype(bf16)

    root = lax.axis_index("z") // (NZ // NX)
    base_full = base_part.astype(f32)
    for shift in (2, 1, 3):
        pairs = []
        for z in range(NZ):
            dst = z // (NZ // NX)
            src = (dst - shift) % NX
            pairs.append((z * NX + src, z * NX + dst))
        got = lax.ppermute(base_part, ("z", "x"), pairs)
        base_full = base_full + got.astype(f32)
    base_full = jnp.where(root == x_here, base_full, 0.0)
    groups = quarter // cols
    place = home % groups

    up = adapter_up_weight.reshape(kept * rank, quarter)

    def terms(k, slots):
        r = rank_full[:, k * half : (k + 1) * half]
        mine = slots[None, :] == my_slots[:, None]
        spread = jnp.where(mine[:, None, :], r[None, :, :], 0).reshape(kept * rank, half)
        delta = lax.dot_general(
            spread.astype(bf16), up, (((0,), (0,)), ((), ())), preferred_element_type=f32
        ).astype(bf16).astype(f32)
        delta = (adapter_scale * delta).reshape(half, groups, cols)
        b = base_full[k * half : (k + 1) * half][:, None, :]
        at = jnp.arange(groups, dtype=jnp.int32)[None, :, None] == place
        return (delta + jnp.where(at, b, 0.0)).astype(bf16).reshape(half, quarter)

    theirs = swap_cores(terms(1, slot_other))
    ours = terms(0, slot_own)
    both = (ours.astype(f32) + theirs.astype(f32)).astype(bf16)
    got_y = lax.all_to_all(both.reshape(NY, NZ * mine_n, quarter), "y", 0, 0, tiled=True)
    sum_y = jnp.sum(got_y.astype(f32), axis=0).astype(bf16)
    got_z = lax.all_to_all(sum_y.reshape(NZ, mine_n, quarter), "z", 0, 0, tiled=True)
    return jnp.sum(got_z.astype(f32), axis=0).astype(bf16)


def solution(mesh):
    fine = Mesh(np.asarray(mesh.devices).reshape(NZ, NY, NC, NX), ("z", "y", "c", "x"))
    return jax.shard_map(
        local,
        mesh=fine,
        in_specs=(
            P(DP, "x"),
            P(DP, "x"),
            P(DP, "x"),
            P(DP, None, "x"),
            P(DP, None, "x"),
            P(DP),
            P(),
            P(),
            P("x", DP),
            P(DP, "x", None),
            P(DP, None, "x"),
        ),
        out_specs=P(DP, "x"),
        check_vma=False,
    )
```

```python
import functools

import jax
import jax.numpy as jnp
import numpy as np
from jax import lax
from jax.experimental import pallas as pl
from jax.experimental.pallas import tpu as pltpu
from jax.sharding import Mesh, PartitionSpec as P

HEAD_SIZE = 128
adapter_scale = 0.5
NZ, NY, NC, NX = 8, 4, 2, 4
DP = ("z", "y", "c")
LANES = 128
MIB = 1 << 20
bf16, f32 = jnp.bfloat16, jnp.float32


def in_hbm(*xs):
    return [pltpu.with_memory_space_constraint(x, pltpu.HBM) for x in xs]


def attend_kernel(
    position, query, fresh_key, fresh_value, keys, values,
    out,
    pos, q_buf, fk_buf, fv_buf, k_buf, v_buf,
    q_rows, probs, fresh_part, o_rows, small_sems, sems,
):
    sessions, cache_len, width = keys.shape
    heads_kv = width // HEAD_SIZE
    heads = query.shape[1] // HEAD_SIZE
    group = heads // heads_kv
    small = [
        pltpu.make_async_copy(src, dst, small_sems.at[i])
        for i, (src, dst) in enumerate(
            ((query, q_buf), (position, pos), (fresh_key, fk_buf), (fresh_value, fv_buf))
        )
    ]
    key_copies = [
        pltpu.make_async_copy(keys.at[s], k_buf.at[s], sems.at[0, s]) for s in range(sessions)
    ]
    value_copies = [
        pltpu.make_async_copy(values.at[s], v_buf.at[s], sems.at[1, s]) for s in range(sessions)
    ]
    for copy in small + key_copies:
        copy.start()

    small[0].wait()
    for h in range(heads):
        q_rows[pl.ds(h, sessions, stride=heads), :] = q_buf[
            :, h * HEAD_SIZE : (h + 1) * HEAD_SIZE
        ].astype(f32)
    for copy in small[1:]:
        copy.wait()
    inverse = HEAD_SIZE ** (-0.5)
    rows_all = sessions * heads
    of_row = lax.broadcasted_iota(jnp.int32, (rows_all, 1), 0)
    kv_of_row = (of_row % heads) // group
    wide = jnp.concatenate(
        [jnp.where(kv_of_row == kv, q_rows[...], 0.0) for kv in range(heads_kv)], axis=1
    )
    wide_low = wide.astype(bf16)
    fresh_keys, fresh_values = fk_buf[...].astype(f32), fv_buf[...].astype(f32)
    fresh_key_rows = []
    fresh_value_rows = []
    for s in range(sessions):
        fresh_key_rows.append(jnp.broadcast_to(fresh_keys[s : s + 1, :], (heads, width)))
        fresh_value_rows.append(jnp.broadcast_to(fresh_values[s : s + 1, :], (heads, width)))
    fresh = (
        jnp.sum(wide * jnp.concatenate(fresh_key_rows, axis=0), axis=1, keepdims=True) * inverse
    )
    values_of_rows = jnp.concatenate(fresh_value_rows, axis=0)
    slots = lax.broadcasted_iota(jnp.int32, (1, cache_len), 1)
    batch = sessions // 2
    for g in range(0, sessions, batch):
        for s in range(g, g + batch):
            key_copies[s].wait()
            value_copies[s].start()
        for s in range(g, g + batch):
            rows = slice(s * heads, (s + 1) * heads)
            scores = lax.dot_general(
                wide_low[rows, :], k_buf[s], (((1,), (1,)), ((), ())), preferred_element_type=f32
            )
            live = (slots < pos[s]) & (slots != lax.rem(pos[s], cache_len))
            scores = jnp.where(live, scores * inverse, jnp.float32(-1e30))
            top = jnp.maximum(jnp.max(scores, axis=1, keepdims=True), fresh[rows, :])
            weights = jnp.exp(scores - top)
            fresh_weight = jnp.exp(fresh[rows, :] - top)
            scale = 1.0 / (jnp.sum(weights, axis=1, keepdims=True) + fresh_weight)
            probs[rows, :] = (weights * scale).astype(bf16)
            fresh_part[rows, :] = (fresh_weight * scale).astype(bf16).astype(
                f32
            ) * values_of_rows[rows, :]
    for g in range(0, sessions, batch):
        for s in range(g, g + batch):
            value_copies[s].wait()
        for s in range(g, g + batch):
            rows = slice(s * heads, (s + 1) * heads)
            both = (
                jnp.dot(probs[rows, :], v_buf[s], preferred_element_type=f32) + fresh_part[rows, :]
            )
            for kv in range(heads_kv):
                o_rows[s * heads + kv * group : s * heads + (kv + 1) * group, :] = both[
                    kv * group : (kv + 1) * group, kv * HEAD_SIZE : (kv + 1) * HEAD_SIZE
                ]
    for h in range(heads):
        rounded = o_rows[pl.ds(h, sessions, stride=heads), :].astype(bf16)
        for k in range(out.shape[0]):
            out[k, :, h * HEAD_SIZE : (h + 1) * HEAD_SIZE] = rounded


def attend(query, incoming_key, incoming_value, keys, values, position, repeats):
    sessions, cache_len, width = keys.shape
    features = query.shape[1]
    heads = features // HEAD_SIZE
    columns = sessions * heads
    anywhere = pl.BlockSpec(memory_space=pl.ANY)
    args = (position, query, incoming_key, incoming_value, keys, values)
    return pl.pallas_call(
        attend_kernel,
        out_shape=jax.ShapeDtypeStruct((repeats, sessions, features), bf16),
        in_specs=[anywhere] * 6,
        out_specs=pl.BlockSpec(memory_space=pltpu.VMEM),
        scratch_shapes=[
            pltpu.SMEM((sessions,), jnp.int32),
            pltpu.VMEM((sessions, features), bf16),
            pltpu.VMEM((sessions, width), bf16),
            pltpu.VMEM((sessions, width), bf16),
            pltpu.VMEM((sessions, cache_len, width), bf16),
            pltpu.VMEM((sessions, cache_len, width), bf16),
            pltpu.VMEM((columns, HEAD_SIZE), f32),
            pltpu.VMEM((columns, cache_len), bf16),
            pltpu.VMEM((columns, width), f32),
            pltpu.VMEM((columns, HEAD_SIZE), f32),
            pltpu.SemaphoreType.DMA((4,)),
            pltpu.SemaphoreType.DMA((2, sessions)),
        ],
        compiler_params=pltpu.CompilerParams(vmem_limit_bytes=14 * MIB),
        cost_estimate=pl.CostEstimate(
            flops=4 * columns * cache_len * width,
            bytes_accessed=4 * sessions * cache_len * width,
            transcendentals=columns * cache_len,
        ),
    )(*in_hbm(*args))


def stage_kernel(*refs):
    count = (len(refs) - 2) // 2
    sources, dests, sems = refs[:count], refs[count + 1 : -1], refs[-1]
    copies = [
        pltpu.make_async_copy(src, dst, sems.at[i])
        for i, (src, dst) in enumerate(zip(sources, dests))
    ]
    for copy in copies:
        copy.start()
    for copy in copies:
        copy.wait()


def stage(arrays, after):
    vmem = pl.BlockSpec(memory_space=pltpu.VMEM)
    anywhere = pl.BlockSpec(memory_space=pl.ANY)
    return pl.pallas_call(
        stage_kernel,
        out_shape=tuple(jax.ShapeDtypeStruct(x.shape, x.dtype) for x in arrays),
        in_specs=[anywhere] * (len(arrays) + 1),
        out_specs=(vmem,) * len(arrays),
        scratch_shapes=[pltpu.SemaphoreType.DMA((len(arrays),))],
        compiler_params=pltpu.CompilerParams(vmem_limit_bytes=8 * MIB),
        cost_estimate=pl.CostEstimate(flops=0, bytes_accessed=8 * MIB, transcendentals=0),
    )(*in_hbm(*arrays), after)


def base_kernel(which, p0, pa, pb, w_own, w_other, base_out):
    piece = p0.shape[0]
    cols = w_own.shape[1]
    rows = jnp.concatenate([p0[...], pa[...], pb[...]], axis=0)
    for i, w in enumerate((w_own, w_other)):
        at = pl.ds(pl.multiple_of(which[i] * cols, LANES), cols)
        base_out[:, at] = jnp.dot(rows, w[...], preferred_element_type=f32).astype(bf16)


def base_terms(which, pieces, w_own, w_other):
    count = sum(p.shape[0] for p in pieces)
    cols = w_own.shape[1]
    vmem = pl.BlockSpec(memory_space=pltpu.VMEM)
    return pl.pallas_call(
        base_kernel,
        out_shape=jax.ShapeDtypeStruct((count, 2 * cols), bf16),
        in_specs=[pl.BlockSpec(memory_space=pltpu.SMEM)] + [vmem] * 5,
        out_specs=vmem,
        compiler_params=pltpu.CompilerParams(vmem_limit_bytes=8 * MIB),
        cost_estimate=pl.CostEstimate(
            flops=4 * count * pieces[0].shape[1] * cols, bytes_accessed=2 * MIB, transcendentals=0
        ),
    )(which, *pieces, w_own, w_other)


def rank_kernel(
    first, which, slots, p0, pa, pb, p2, down_own, down_other, w_own, w_other, after, out, rows
):
    piece = p0.shape[0]
    for k, p in enumerate((p0, pa, pb, p2)):
        rows[k * piece : (k + 1) * piece, :] = p[...]
    kept, rank, features = down_own.shape
    cols = w_own.shape[1]
    acc = jnp.zeros((rank, slots.shape[1]), f32)
    for i, down in enumerate((down_own, down_other)):
        portion = lax.dot_general(
            down[...].reshape(kept * rank, features),
            rows[...],
            (((1,), (1,)), ((), ())),
            preferred_element_type=f32,
        )
        for j in range(kept):
            acc = acc + jnp.where(
                slots[...] == first[i] + j, portion[j * rank : (j + 1) * rank, :], 0.0
            )
    out[:rank, :] = acc.astype(bf16)
    for i, w in enumerate((w_own, w_other)):
        at = pl.ds(pl.multiple_of(which[i] * cols, LANES), cols)
        out[rank:, at] = jnp.dot(p2[...], w[...], preferred_element_type=f32).astype(bf16)


def rank_terms(first, which, slots, pieces, down_own, down_other, w_own, w_other, after):
    count = slots.shape[1]
    piece, features = pieces[0].shape
    kept, rank, features = down_own.shape
    vmem = pl.BlockSpec(memory_space=pltpu.VMEM)
    smem = pl.BlockSpec(memory_space=pltpu.SMEM)
    return pl.pallas_call(
        rank_kernel,
        out_shape=jax.ShapeDtypeStruct((rank + piece, count), bf16),
        in_specs=[smem, smem] + [vmem] * 9 + [pl.BlockSpec(memory_space=pl.ANY)],
        out_specs=vmem,
        scratch_shapes=[pltpu.VMEM((count, features), bf16)],
        compiler_params=pltpu.CompilerParams(vmem_limit_bytes=12 * MIB),
        cost_estimate=pl.CostEstimate(
            flops=4 * count * features * kept * rank, bytes_accessed=6 * MIB, transcendentals=0
        ),
    )(first, which, slots, *pieces, down_own, down_other, w_own, w_other, after)


def expand_kernel(first, slots, r0, r1, r2, r3, up_own, up_other, o0, oa, ob, o2, spread):
    outs = (o0, oa, ob, o2)
    count = slots.shape[1]
    kept_rank, quarter = up_own.shape
    piece = o0.shape[0]
    rank = r0.shape[0] - piece
    summed = (r0[...].astype(f32) + r1[...].astype(f32)) + (
        r2[...].astype(f32) + r3[...].astype(f32)
    )
    ranks = summed[:rank, :].T
    both = jnp.concatenate([ranks, ranks], axis=1)
    slot_rows = jnp.broadcast_to(slots[...].astype(f32), (LANES, count)).T
    part = lax.broadcasted_iota(jnp.int32, (1, LANES), 1) // rank
    for which in range(2):
        for j in range(kept_rank // LANES):
            slot = (first[which] + 2 * j + part).astype(f32)
            at = which * kept_rank + j * LANES
            spread[:, at : at + LANES] = jnp.where(slot_rows == slot, both, 0.0).astype(bf16)
    step = 512
    for n in range(0, quarter, step):
        cols = slice(n, n + step)
        delta = jnp.dot(
            spread[:, :kept_rank], up_own[:, cols], preferred_element_type=f32
        ) + jnp.dot(spread[:, kept_rank:], up_other[:, cols], preferred_element_type=f32)
        delta = (adapter_scale * delta.astype(bf16).astype(f32)).astype(bf16)
        for k, o in enumerate(outs):
            o[:, cols] = delta[k * piece : (k + 1) * piece, :]

    @pl.when(first[3] == 1)
    def _():
        at = pl.ds(pl.multiple_of(first[2], LANES), count)
        o2[:, at] = (o2[:, at].astype(f32) + summed[rank:, :]).astype(bf16)


def expand(first, slots, ranks, up_own, up_other):
    count = slots.shape[1]
    kept_rank, quarter = up_own.shape
    piece = count // NY
    vmem = pl.BlockSpec(memory_space=pltpu.VMEM)
    smem = pl.BlockSpec(memory_space=pltpu.SMEM)
    return pl.pallas_call(
        expand_kernel,
        out_shape=(jax.ShapeDtypeStruct((piece, quarter), bf16),) * 4,
        in_specs=[smem] + [vmem] * 7,
        out_specs=(vmem,) * 4,
        scratch_shapes=[pltpu.VMEM((count, 2 * kept_rank), bf16)],
        compiler_params=pltpu.CompilerParams(vmem_limit_bytes=12 * MIB),
        cost_estimate=pl.CostEstimate(
            flops=4 * count * kept_rank * quarter, bytes_accessed=6 * MIB, transcendentals=0
        ),
    )(first, slots, *ranks, up_own, up_other)


def join_kernel(place, d0, ea, eb, b0, b1, b2, out):
    out[...] = ((d0[...].astype(f32) + ea[...].astype(f32)) + eb[...].astype(f32)).astype(bf16)

    @pl.when(place[3] == 1)
    def _():
        cols = b0.shape[1]
        for i, b in enumerate((b0, b1, b2)):
            at = pl.ds(pl.multiple_of(place[i], LANES), cols)
            total = (d0[:, at].astype(f32) + ea[:, at].astype(f32)) + eb[:, at].astype(f32)
            out[:, at] = (total + b[...].astype(f32)).astype(bf16)


def join(place, rows, bases):
    vmem = pl.BlockSpec(memory_space=pltpu.VMEM)
    return pl.pallas_call(
        join_kernel,
        out_shape=jax.ShapeDtypeStruct(rows[0].shape, bf16),
        in_specs=[pl.BlockSpec(memory_space=pltpu.SMEM)] + [vmem] * 6,
        out_specs=vmem,
        compiler_params=pltpu.CompilerParams(vmem_limit_bytes=8 * MIB),
        cost_estimate=pl.CostEstimate(flops=MIB, bytes_accessed=MIB, transcendentals=0),
    )(place, *rows, *bases)


def swap_cores(x):
    return lax.ppermute(x, "c", [(0, 1), (1, 0)])


def along_y(x, way):
    pairs = []
    for y in range(NY):
        for c in range(NC):
            step = way if c == 0 else -way
            pairs.append((y * NC + c, ((y + step) % NY) * NC + c))
    return lax.ppermute(x, ("y", "c"), pairs)


def to_root(x, shift):
    pairs = []
    for z in range(NZ):
        owner = z // (NZ // NX)
        pairs.append((z * NX + (owner - shift) % NX, z * NX + owner))
    return lax.ppermute(x, ("z", "x"), pairs)


def along_x(x, shift):
    return lax.ppermute(x, "x", [(i, (i + shift) % NX) for i in range(NX)])


def local(
    query,
    incoming_key,
    incoming_value,
    cycle_key_cache,
    cycle_value_cache,
    position,
    tenant,
    tenant_adapter_index,
    output_weight,
    adapter_down_weight,
    adapter_up_weight,
):
    kept, features, rank = adapter_down_weight.shape
    cols = output_weight.shape[1]
    quarter = adapter_up_weight.shape[2]
    mine_n = query.shape[0]
    block = NZ * mine_n
    z_here, y_here, core, x_here = (lax.axis_index(a) for a in ("z", "y", "c", "x"))
    home = (z_here * NY + y_here) * NC + core
    other = home + 1 - 2 * core
    down = jnp.swapaxes(adapter_down_weight, 1, 2)
    up = adapter_up_weight.reshape(kept * rank, quarter)

    copies = attend(
        query,
        incoming_key,
        incoming_value,
        cycle_key_cache,
        cycle_value_cache,
        position,
        NZ,
    )
    copies, down, up, output_weight = lax.optimization_barrier((copies, down, up, output_weight))
    down_other = swap_cores(down)
    w_other = swap_cores(output_weight)
    up_other = swap_cores(up)
    p0 = lax.all_to_all(copies, "z", 0, 0, tiled=True).reshape(block, features)

    pa = along_y(p0, 1)
    pb = along_y(p0, -1)
    p2 = along_y(pa, 1)

    tenants_all = tenant_adapter_index.shape[0]
    matches = tenant[:, None] == jnp.arange(tenants_all, dtype=jnp.int32)[None, :]
    slot_of = jnp.sum(jnp.where(matches, tenant_adapter_index[None, :], 0), axis=1)
    table = slot_of.reshape(NZ, NY, NC, mine_n).transpose(2, 1, 0, 3).reshape(NC * NY, block)
    ahead = 1 - 2 * core
    ys = jnp.stack([y_here, y_here - ahead, y_here + ahead, y_here + 2]) % NY
    pick = (ys + core * NY)[:, None] == jnp.arange(NC * NY, dtype=jnp.int32)[None, :]
    slots = jnp.sum(jnp.where(pick[:, :, None], table[None], 0), axis=1).reshape(1, NY * block)

    add = lambda *xs: functools.reduce(jnp.add, [x.astype(f32) for x in xs]).astype(bf16)
    is_root = (x_here == z_here // (NZ // NX)).astype(jnp.int32)
    width = NC * cols
    columns = (z_here % (NZ // NX)) * NY
    which = jnp.stack([core, 1 - core])
    first = jnp.stack([home * kept, other * kept, (columns + y_here) * width, is_root])

    (down_other,) = stage((down_other,), p0)
    base_part = base_terms(which, (p0, pa, pb), output_weight, w_other)
    sums = [base_part] + [to_root(base_part, s) for s in (2, 1, 3)]
    packed = rank_terms(
        first, which, slots, (p0, pa, pb, p2), down, down_other, output_weight, w_other, base_part
    )
    packs = [packed] + [along_x(packed, s) for s in (1, 3, 2)]
    base = add(*sums).reshape(NY - 1, block, width)
    bases = [base[0], along_y(base[1], -1), along_y(base[2], 1)]
    senders = jnp.stack([y_here, y_here + ahead, y_here - ahead]) % NY
    place = jnp.concatenate([(columns + senders) * width, is_root[None]])

    ups = stage((up, up_other), packed)
    d0, da, db, d2 = expand(first, slots, packs, *ups)

    e2 = along_y(d2, 1)
    ea = along_y(da, -1)
    eb = along_y(add(db, e2), 1)
    home_rows = join(place, (d0, ea, eb), bases)
    got = lax.all_to_all(home_rows.reshape(NZ, mine_n, quarter), "z", 0, 0, tiled=True)
    return jnp.sum(got.astype(f32), axis=0).astype(bf16)


def solution(mesh):
    fine = Mesh(np.asarray(mesh.devices).reshape(NZ, NY, NC, NX), DP + ("x",))
    return jax.shard_map(
        local,
        mesh=fine,
        in_specs=(
            P(DP, "x"),
            P(DP, "x"),
            P(DP, "x"),
            P(DP, None, "x"),
            P(DP, None, "x"),
            P(DP),
            P(),
            P(),
            P("x", DP),
            P(DP, "x", None),
            P(DP, None, "x"),
        ),
        out_specs=P(DP, "x"),
        check_vma=False,
    )
```

```python
import functools

import jax
import jax.numpy as jnp
import numpy as np
from jax import lax
from jax.experimental import pallas as pl
from jax.experimental.pallas import tpu as pltpu
from jax.sharding import Mesh, PartitionSpec as P

HEAD_SIZE = 128
adapter_scale = 0.5
NZ, NY, NC, NX = 8, 4, 2, 4
DP = ("z", "y", "c")
LANES = 128
MIB = 1 << 20
bf16, f32 = jnp.bfloat16, jnp.float32


def in_hbm(*xs):
    return [pltpu.with_memory_space_constraint(x, pltpu.HBM) for x in xs]


def attend_kernel(
    position, query, fresh_key, fresh_value, keys, values,
    out,
    pos, q_buf, fk_buf, fv_buf, k_buf, v_buf,
    q_rows, probs, fresh_part, o_rows, small_sems, sems,
):
    sessions, cache_len, width = keys.shape
    heads_kv = width // HEAD_SIZE
    heads = query.shape[1] // HEAD_SIZE
    group = heads // heads_kv
    small = [
        pltpu.make_async_copy(src, dst, small_sems.at[i])
        for i, (src, dst) in enumerate(
            ((query, q_buf), (position, pos), (fresh_key, fk_buf), (fresh_value, fv_buf))
        )
    ]
    key_copies = [
        pltpu.make_async_copy(keys.at[s], k_buf.at[s], sems.at[0, s]) for s in range(sessions)
    ]
    value_copies = [
        pltpu.make_async_copy(values.at[s], v_buf.at[s], sems.at[1, s]) for s in range(sessions)
    ]
    for copy in small + key_copies:
        copy.start()

    small[0].wait()
    for h in range(heads):
        q_rows[pl.ds(h, sessions, stride=heads), :] = q_buf[
            :, h * HEAD_SIZE : (h + 1) * HEAD_SIZE
        ].astype(f32)
    for copy in small[1:]:
        copy.wait()
    inverse = HEAD_SIZE ** (-0.5)
    rows_all = sessions * heads
    of_row = lax.broadcasted_iota(jnp.int32, (rows_all, 1), 0)
    kv_of_row = (of_row % heads) // group
    wide = jnp.concatenate(
        [jnp.where(kv_of_row == kv, q_rows[...], 0.0) for kv in range(heads_kv)], axis=1
    )
    wide_low = wide.astype(bf16)
    fresh_keys, fresh_values = fk_buf[...].astype(f32), fv_buf[...].astype(f32)
    fresh_key_rows = []
    fresh_value_rows = []
    for s in range(sessions):
        fresh_key_rows.append(jnp.broadcast_to(fresh_keys[s : s + 1, :], (heads, width)))
        fresh_value_rows.append(jnp.broadcast_to(fresh_values[s : s + 1, :], (heads, width)))
    fresh = (
        jnp.sum(wide * jnp.concatenate(fresh_key_rows, axis=0), axis=1, keepdims=True) * inverse
    )
    values_of_rows = jnp.concatenate(fresh_value_rows, axis=0)
    slots = lax.broadcasted_iota(jnp.int32, (1, cache_len), 1)
    batch = sessions // 2
    for g in range(0, sessions, batch):
        for s in range(g, g + batch):
            key_copies[s].wait()
            value_copies[s].start()
        for s in range(g, g + batch):
            rows = slice(s * heads, (s + 1) * heads)
            scores = lax.dot_general(
                wide_low[rows, :], k_buf[s], (((1,), (1,)), ((), ())), preferred_element_type=f32
            )
            live = (slots < pos[s]) & (slots != lax.rem(pos[s], cache_len))
            scores = jnp.where(live, scores * inverse, jnp.float32(-1e30))
            top = jnp.maximum(jnp.max(scores, axis=1, keepdims=True), fresh[rows, :])
            weights = jnp.exp(scores - top)
            fresh_weight = jnp.exp(fresh[rows, :] - top)
            scale = 1.0 / (jnp.sum(weights, axis=1, keepdims=True) + fresh_weight)
            probs[rows, :] = (weights * scale).astype(bf16)
            fresh_part[rows, :] = (fresh_weight * scale).astype(bf16).astype(
                f32
            ) * values_of_rows[rows, :]
    for g in range(0, sessions, batch):
        for s in range(g, g + batch):
            value_copies[s].wait()
        for s in range(g, g + batch):
            rows = slice(s * heads, (s + 1) * heads)
            both = (
                jnp.dot(probs[rows, :], v_buf[s], preferred_element_type=f32) + fresh_part[rows, :]
            )
            for kv in range(heads_kv):
                o_rows[s * heads + kv * group : s * heads + (kv + 1) * group, :] = both[
                    kv * group : (kv + 1) * group, kv * HEAD_SIZE : (kv + 1) * HEAD_SIZE
                ]
    for h in range(heads):
        rounded = o_rows[pl.ds(h, sessions, stride=heads), :].astype(bf16)
        for k in range(out.shape[0]):
            out[k, :, h * HEAD_SIZE : (h + 1) * HEAD_SIZE] = rounded


def attend(query, incoming_key, incoming_value, keys, values, position, repeats):
    sessions, cache_len, width = keys.shape
    features = query.shape[1]
    heads = features // HEAD_SIZE
    columns = sessions * heads
    anywhere = pl.BlockSpec(memory_space=pl.ANY)
    args = (position, query, incoming_key, incoming_value, keys, values)
    return pl.pallas_call(
        attend_kernel,
        out_shape=jax.ShapeDtypeStruct((repeats, sessions, features), bf16),
        in_specs=[anywhere] * 6,
        out_specs=pl.BlockSpec(memory_space=pltpu.VMEM),
        scratch_shapes=[
            pltpu.SMEM((sessions,), jnp.int32),
            pltpu.VMEM((sessions, features), bf16),
            pltpu.VMEM((sessions, width), bf16),
            pltpu.VMEM((sessions, width), bf16),
            pltpu.VMEM((sessions, cache_len, width), bf16),
            pltpu.VMEM((sessions, cache_len, width), bf16),
            pltpu.VMEM((columns, HEAD_SIZE), f32),
            pltpu.VMEM((columns, cache_len), bf16),
            pltpu.VMEM((columns, width), f32),
            pltpu.VMEM((columns, HEAD_SIZE), f32),
            pltpu.SemaphoreType.DMA((4,)),
            pltpu.SemaphoreType.DMA((2, sessions)),
        ],
        compiler_params=pltpu.CompilerParams(vmem_limit_bytes=14 * MIB),
        cost_estimate=pl.CostEstimate(
            flops=4 * columns * cache_len * width,
            bytes_accessed=4 * sessions * cache_len * width,
            transcendentals=columns * cache_len,
        ),
    )(*in_hbm(*args))


def stage_kernel(*refs):
    count = (len(refs) - 2) // 2
    sources, dests, sems = refs[:count], refs[count + 1 : -1], refs[-1]
    copies = [
        pltpu.make_async_copy(src, dst, sems.at[i])
        for i, (src, dst) in enumerate(zip(sources, dests))
    ]
    for copy in copies:
        copy.start()
    for copy in copies:
        copy.wait()


def stage(arrays, after):
    vmem = pl.BlockSpec(memory_space=pltpu.VMEM)
    anywhere = pl.BlockSpec(memory_space=pl.ANY)
    return pl.pallas_call(
        stage_kernel,
        out_shape=tuple(jax.ShapeDtypeStruct(x.shape, x.dtype) for x in arrays),
        in_specs=[anywhere] * (len(arrays) + 1),
        out_specs=(vmem,) * len(arrays),
        scratch_shapes=[pltpu.SemaphoreType.DMA((len(arrays),))],
        compiler_params=pltpu.CompilerParams(vmem_limit_bytes=8 * MIB),
        cost_estimate=pl.CostEstimate(flops=0, bytes_accessed=8 * MIB, transcendentals=0),
    )(*in_hbm(*arrays), after)


def base_kernel(which, p0, pa, pb, w_own, w_other, base_out):
    piece = p0.shape[0]
    cols = w_own.shape[1]
    rows = jnp.concatenate([p0[...], pa[...], pb[...]], axis=0)
    for i, w in enumerate((w_own, w_other)):
        at = pl.ds(pl.multiple_of(which[i] * cols, LANES), cols)
        base_out[:, at] = jnp.dot(rows, w[...], preferred_element_type=f32).astype(bf16)


def base_terms(which, pieces, w_own, w_other):
    count = sum(p.shape[0] for p in pieces)
    cols = w_own.shape[1]
    vmem = pl.BlockSpec(memory_space=pltpu.VMEM)
    return pl.pallas_call(
        base_kernel,
        out_shape=jax.ShapeDtypeStruct((count, 2 * cols), bf16),
        in_specs=[pl.BlockSpec(memory_space=pltpu.SMEM)] + [vmem] * 5,
        out_specs=vmem,
        compiler_params=pltpu.CompilerParams(vmem_limit_bytes=8 * MIB),
        cost_estimate=pl.CostEstimate(
            flops=4 * count * pieces[0].shape[1] * cols, bytes_accessed=2 * MIB, transcendentals=0
        ),
    )(which, *pieces, w_own, w_other)


def rank_kernel(
    first, which, slots, p0, pa, pb, p2, down_own, down_other, w_own, w_other, after, out, rows
):
    piece = p0.shape[0]
    for k, p in enumerate((p0, pa, pb, p2)):
        rows[k * piece : (k + 1) * piece, :] = p[...]
    kept, rank, features = down_own.shape
    cols = w_own.shape[1]
    acc = jnp.zeros((rank, slots.shape[1]), f32)
    for i, down in enumerate((down_own, down_other)):
        portion = lax.dot_general(
            down[...].reshape(kept * rank, features),
            rows[...],
            (((1,), (1,)), ((), ())),
            preferred_element_type=f32,
        )
        for j in range(kept):
            acc = acc + jnp.where(
                slots[...] == first[i] + j, portion[j * rank : (j + 1) * rank, :], 0.0
            )
    out[:rank, :] = acc.astype(bf16)
    for i, w in enumerate((w_own, w_other)):
        at = pl.ds(pl.multiple_of(which[i] * cols, LANES), cols)
        out[rank:, at] = jnp.dot(p2[...], w[...], preferred_element_type=f32).astype(bf16)


def rank_terms(first, which, slots, pieces, down_own, down_other, w_own, w_other, after):
    count = slots.shape[1]
    piece, features = pieces[0].shape
    kept, rank, features = down_own.shape
    vmem = pl.BlockSpec(memory_space=pltpu.VMEM)
    smem = pl.BlockSpec(memory_space=pltpu.SMEM)
    return pl.pallas_call(
        rank_kernel,
        out_shape=jax.ShapeDtypeStruct((rank + piece, count), bf16),
        in_specs=[smem, smem] + [vmem] * 9 + [pl.BlockSpec(memory_space=pl.ANY)],
        out_specs=vmem,
        scratch_shapes=[pltpu.VMEM((count, features), bf16)],
        compiler_params=pltpu.CompilerParams(vmem_limit_bytes=12 * MIB),
        cost_estimate=pl.CostEstimate(
            flops=4 * count * features * kept * rank, bytes_accessed=6 * MIB, transcendentals=0
        ),
    )(first, which, slots, *pieces, down_own, down_other, w_own, w_other, after)


def scaled_rows(spread, up_own, up_other, outs):
    kept_rank, quarter = up_own.shape
    piece = outs[0].shape[0]
    step = 512
    for n in range(0, quarter, step):
        cols = slice(n, n + step)
        delta = jnp.dot(
            spread[:, :kept_rank], up_own[:, cols], preferred_element_type=f32
        ) + jnp.dot(spread[:, kept_rank:], up_other[:, cols], preferred_element_type=f32)
        delta = (adapter_scale * delta.astype(bf16).astype(f32)).astype(bf16)
        for k, o in enumerate(outs):
            o[:, cols] = delta[k * piece : (k + 1) * piece, :]


def expand_last_kernel(first, slots, r0, r1, r2, r3, up_own, up_other, o2, spread, spread2):
    count = slots.shape[1]
    kept_rank = up_own.shape[0]
    piece = o2.shape[0]
    rank = r0.shape[0] - piece
    head = count - piece
    summed = (r0[...].astype(f32) + r1[...].astype(f32)) + (
        r2[...].astype(f32) + r3[...].astype(f32)
    )
    ranks = summed[:rank, :].T
    both = jnp.concatenate([ranks, ranks], axis=1)
    slot_rows = jnp.broadcast_to(slots[...].astype(f32), (LANES, count)).T
    part = lax.broadcasted_iota(jnp.int32, (1, LANES), 1) // rank
    for which in range(2):
        for j in range(kept_rank // LANES):
            slot = (first[which] + 2 * j + part).astype(f32)
            at = which * kept_rank + j * LANES
            block = jnp.where(slot_rows == slot, both, 0.0).astype(bf16)
            spread[:, at : at + LANES] = block[:head, :]
            spread2[:, at : at + LANES] = block[head:, :]
    scaled_rows(spread2, up_own, up_other, (o2,))

    @pl.when(first[3] == 1)
    def _():
        at = pl.ds(pl.multiple_of(first[2], LANES), count)
        o2[:, at] = (o2[:, at].astype(f32) + summed[rank:, :]).astype(bf16)


def expand_last(first, slots, ranks, up_own, up_other):
    count = slots.shape[1]
    kept_rank, quarter = up_own.shape
    piece = count // NY
    vmem = pl.BlockSpec(memory_space=pltpu.VMEM)
    smem = pl.BlockSpec(memory_space=pltpu.SMEM)
    return pl.pallas_call(
        expand_last_kernel,
        out_shape=(
            jax.ShapeDtypeStruct((piece, quarter), bf16),
            jax.ShapeDtypeStruct((count - piece, 2 * kept_rank), bf16),
        ),
        in_specs=[smem] + [vmem] * 7,
        out_specs=(vmem,) * 2,
        scratch_shapes=[pltpu.VMEM((piece, 2 * kept_rank), bf16)],
        compiler_params=pltpu.CompilerParams(vmem_limit_bytes=10 * MIB),
        cost_estimate=pl.CostEstimate(
            flops=4 * piece * kept_rank * quarter, bytes_accessed=4 * MIB, transcendentals=0
        ),
    )(first, slots, *ranks, up_own, up_other)


def expand_kernel(first, spread, up_own, up_other, base, *outs):
    scaled_rows(spread, up_own, up_other, outs)

    @pl.when(first[3] == 1)
    def _():
        piece = outs[0].shape[0]
        at = pl.ds(pl.multiple_of(first[2], LANES), base.shape[1])
        for k, o in enumerate(outs):
            o[:, at] = (o[:, at].astype(f32) + base[k * piece : (k + 1) * piece, :]).astype(bf16)


def expand(first, spread, up_own, up_other, base):
    quarter = up_own.shape[1]
    piece = spread.shape[0] // (NY - 1)
    vmem = pl.BlockSpec(memory_space=pltpu.VMEM)
    return pl.pallas_call(
        expand_kernel,
        out_shape=(jax.ShapeDtypeStruct((piece, quarter), bf16),) * (NY - 1),
        in_specs=[pl.BlockSpec(memory_space=pltpu.SMEM)] + [vmem] * 4,
        out_specs=(vmem,) * (NY - 1),
        compiler_params=pltpu.CompilerParams(vmem_limit_bytes=10 * MIB),
        cost_estimate=pl.CostEstimate(
            flops=2 * spread.size * quarter, bytes_accessed=5 * MIB, transcendentals=0
        ),
    )(first, spread, up_own, up_other, base)


def gather_kernel(up_own, up_other, b0, b1, b2, b3, after, own_out, other_out, base_out, sems):
    copies = [
        pltpu.make_async_copy(src, dst, sems.at[i])
        for i, (src, dst) in enumerate(((up_own, own_out), (up_other, other_out)))
    ]
    for copy in copies:
        copy.start()
    base_out[...] = (b0[...].astype(f32) + b1[...].astype(f32)) + (
        b2[...].astype(f32) + b3[...].astype(f32)
    )
    for copy in copies:
        copy.wait()


def gather_ups(up_own, up_other, parts, after):
    vmem = pl.BlockSpec(memory_space=pltpu.VMEM)
    anywhere = pl.BlockSpec(memory_space=pl.ANY)
    return pl.pallas_call(
        gather_kernel,
        out_shape=(
            jax.ShapeDtypeStruct(up_own.shape, bf16),
            jax.ShapeDtypeStruct(up_other.shape, bf16),
            jax.ShapeDtypeStruct(parts[0].shape, f32),
        ),
        in_specs=[anywhere] * 2 + [vmem] * NX + [anywhere],
        out_specs=(vmem,) * 3,
        scratch_shapes=[pltpu.SemaphoreType.DMA((2,))],
        compiler_params=pltpu.CompilerParams(vmem_limit_bytes=10 * MIB),
        cost_estimate=pl.CostEstimate(flops=MIB, bytes_accessed=8 * MIB, transcendentals=0),
    )(*in_hbm(up_own, up_other), *parts, after)


def swap_cores(x):
    return lax.ppermute(x, "c", [(0, 1), (1, 0)])


def along_y(x, way):
    pairs = []
    for y in range(NY):
        for c in range(NC):
            step = way if c == 0 else -way
            pairs.append((y * NC + c, ((y + step) % NY) * NC + c))
    return lax.ppermute(x, ("y", "c"), pairs)


def to_root(x, shift):
    pairs = []
    for z in range(NZ):
        owner = z // (NZ // NX)
        pairs.append((z * NX + (owner - shift) % NX, z * NX + owner))
    return lax.ppermute(x, ("z", "x"), pairs)


def along_x(x, shift):
    return lax.ppermute(x, "x", [(i, (i + shift) % NX) for i in range(NX)])


def local(
    query,
    incoming_key,
    incoming_value,
    cycle_key_cache,
    cycle_value_cache,
    position,
    tenant,
    tenant_adapter_index,
    output_weight,
    adapter_down_weight,
    adapter_up_weight,
):
    kept, features, rank = adapter_down_weight.shape
    cols = output_weight.shape[1]
    quarter = adapter_up_weight.shape[2]
    mine_n = query.shape[0]
    block = NZ * mine_n
    z_here, y_here, core, x_here = (lax.axis_index(a) for a in ("z", "y", "c", "x"))
    home = (z_here * NY + y_here) * NC + core
    other = home + 1 - 2 * core
    down = jnp.swapaxes(adapter_down_weight, 1, 2)
    up = adapter_up_weight.reshape(kept * rank, quarter)

    copies = attend(
        query,
        incoming_key,
        incoming_value,
        cycle_key_cache,
        cycle_value_cache,
        position,
        NZ,
    )
    down_other = swap_cores(down)
    w_other = swap_cores(output_weight)
    up_other = swap_cores(up)
    p0 = lax.all_to_all(copies, "z", 0, 0, tiled=True).reshape(block, features)

    tenants_all = tenant_adapter_index.shape[0]
    matches = tenant[:, None] == jnp.arange(tenants_all, dtype=jnp.int32)[None, :]
    slot_of = jnp.sum(jnp.where(matches, tenant_adapter_index[None, :], 0), axis=1)
    table = slot_of.reshape(NZ, NY, NC, mine_n).transpose(2, 1, 0, 3).reshape(NC * NY, block)
    ahead = 1 - 2 * core
    ys = jnp.stack([y_here, y_here - ahead, y_here + ahead, y_here + 2]) % NY
    pick = (ys + core * NY)[:, None] == jnp.arange(NC * NY, dtype=jnp.int32)[None, :]
    slots = jnp.sum(jnp.where(pick[:, :, None], table[None], 0), axis=1).reshape(1, NY * block)

    pa = along_y(p0, 1)
    pb = along_y(p0, -1)
    p2 = along_y(pa, 1)

    add = lambda *xs: functools.reduce(jnp.add, [x.astype(f32) for x in xs]).astype(bf16)
    is_root = (x_here == z_here // (NZ // NX)).astype(jnp.int32)
    width = NC * cols
    columns = (z_here % (NZ // NX)) * NY
    which = jnp.stack([core, 1 - core])
    first = jnp.stack([home * kept, other * kept, (columns + y_here) * width, is_root])

    (down_other,) = stage((down_other,), p0)
    base_part = base_terms(which, (p0, pa, pb), output_weight, w_other)
    packed = rank_terms(
        first, which, slots, (p0, pa, pb, p2), down, down_other, output_weight, w_other, base_part
    )
    packs = [packed] + [along_x(packed, s) for s in (1, 3, 2)]
    sums = [base_part] + [to_root(base_part, s) for s in (2, 1, 3)]
    *ups, base = gather_ups(up, up_other, sums, packed)
    d2, spread = expand_last(first, slots, packs, *ups)
    e2 = along_y(d2, 1)
    d0, da, db = expand(first, spread, *ups, base)

    ea = along_y(da, -1)
    eb = along_y(add(db, e2), 1)
    home_rows = add(d0, ea, eb)
    got = lax.all_to_all(home_rows.reshape(NZ, mine_n, quarter), "z", 0, 0, tiled=True)
    return jnp.sum(got.astype(f32), axis=0).astype(bf16)


def solution(mesh):
    fine = Mesh(np.asarray(mesh.devices).reshape(NZ, NY, NC, NX), DP + ("x",))
    return jax.shard_map(
        local,
        mesh=fine,
        in_specs=(
            P(DP, "x"),
            P(DP, "x"),
            P(DP, "x"),
            P(DP, None, "x"),
            P(DP, None, "x"),
            P(DP),
            P(),
            P(),
            P("x", DP),
            P(DP, "x", None),
            P(DP, None, "x"),
        ),
        out_specs=P(DP, "x"),
        check_vma=False,
    )
```

```python
import functools

import jax
import jax.numpy as jnp
import numpy as np
from jax import lax
from jax.experimental import pallas as pl
from jax.experimental.pallas import tpu as pltpu
from jax.sharding import Mesh, PartitionSpec as P

HEAD_SIZE = 128
adapter_scale = 0.5
NZ, NY, NC, NX = 8, 4, 2, 4
DP = ("z", "y", "c")
LANES = 128
MIB = 1 << 20
bf16, f32 = jnp.bfloat16, jnp.float32


def in_hbm(*xs):
    return [pltpu.with_memory_space_constraint(x, pltpu.HBM) for x in xs]


def attend_kernel(
    position, query, fresh_key, fresh_value, keys, values,
    out,
    pos, q_buf, fk_buf, fv_buf, k_buf, v_buf,
    q_rows, probs, fresh_part, o_rows, small_sems, sems,
):
    sessions, cache_len, width = keys.shape
    heads_kv = width // HEAD_SIZE
    heads = query.shape[1] // HEAD_SIZE
    group = heads // heads_kv
    small = [
        pltpu.make_async_copy(src, dst, small_sems.at[i])
        for i, (src, dst) in enumerate(
            ((query, q_buf), (position, pos), (fresh_key, fk_buf), (fresh_value, fv_buf))
        )
    ]
    key_copies = [
        pltpu.make_async_copy(keys.at[s], k_buf.at[s], sems.at[0, s]) for s in range(sessions)
    ]
    value_copies = [
        pltpu.make_async_copy(values.at[s], v_buf.at[s], sems.at[1, s]) for s in range(sessions)
    ]
    for copy in small + key_copies:
        copy.start()

    small[0].wait()
    for h in range(heads):
        q_rows[pl.ds(h, sessions, stride=heads), :] = q_buf[
            :, h * HEAD_SIZE : (h + 1) * HEAD_SIZE
        ].astype(f32)
    for copy in small[1:]:
        copy.wait()
    inverse = HEAD_SIZE ** (-0.5)
    rows_all = sessions * heads
    of_row = lax.broadcasted_iota(jnp.int32, (rows_all, 1), 0)
    kv_of_row = (of_row % heads) // group
    wide = jnp.concatenate(
        [jnp.where(kv_of_row == kv, q_rows[...], 0.0) for kv in range(heads_kv)], axis=1
    )
    wide_low = wide.astype(bf16)
    fresh_keys, fresh_values = fk_buf[...].astype(f32), fv_buf[...].astype(f32)
    fresh_key_rows = []
    fresh_value_rows = []
    for s in range(sessions):
        fresh_key_rows.append(jnp.broadcast_to(fresh_keys[s : s + 1, :], (heads, width)))
        fresh_value_rows.append(jnp.broadcast_to(fresh_values[s : s + 1, :], (heads, width)))
    fresh = (
        jnp.sum(wide * jnp.concatenate(fresh_key_rows, axis=0), axis=1, keepdims=True) * inverse
    )
    values_of_rows = jnp.concatenate(fresh_value_rows, axis=0)
    slots = lax.broadcasted_iota(jnp.int32, (1, cache_len), 1)
    batch = sessions // 2
    for g in range(0, sessions, batch):
        for s in range(g, g + batch):
            key_copies[s].wait()
            value_copies[s].start()
        for s in range(g, g + batch):
            rows = slice(s * heads, (s + 1) * heads)
            scores = lax.dot_general(
                wide_low[rows, :], k_buf[s], (((1,), (1,)), ((), ())), preferred_element_type=f32
            )
            live = (slots < pos[s]) & (slots != lax.rem(pos[s], cache_len))
            scores = jnp.where(live, scores * inverse, jnp.float32(-1e30))
            top = jnp.maximum(jnp.max(scores, axis=1, keepdims=True), fresh[rows, :])
            weights = jnp.exp(scores - top)
            fresh_weight = jnp.exp(fresh[rows, :] - top)
            scale = 1.0 / (jnp.sum(weights, axis=1, keepdims=True) + fresh_weight)
            probs[rows, :] = (weights * scale).astype(bf16)
            fresh_part[rows, :] = (fresh_weight * scale).astype(bf16).astype(
                f32
            ) * values_of_rows[rows, :]
    for g in range(0, sessions, batch):
        for s in range(g, g + batch):
            value_copies[s].wait()
        for s in range(g, g + batch):
            rows = slice(s * heads, (s + 1) * heads)
            both = (
                jnp.dot(probs[rows, :], v_buf[s], preferred_element_type=f32) + fresh_part[rows, :]
            )
            for kv in range(heads_kv):
                o_rows[s * heads + kv * group : s * heads + (kv + 1) * group, :] = both[
                    kv * group : (kv + 1) * group, kv * HEAD_SIZE : (kv + 1) * HEAD_SIZE
                ]
    for h in range(heads):
        rounded = o_rows[pl.ds(h, sessions, stride=heads), :].astype(bf16)
        for k in range(out.shape[0]):
            out[k, :, h * HEAD_SIZE : (h + 1) * HEAD_SIZE] = rounded


def attend(query, incoming_key, incoming_value, keys, values, position, repeats):
    sessions, cache_len, width = keys.shape
    features = query.shape[1]
    heads = features // HEAD_SIZE
    columns = sessions * heads
    anywhere = pl.BlockSpec(memory_space=pl.ANY)
    args = (position, query, incoming_key, incoming_value, keys, values)
    return pl.pallas_call(
        attend_kernel,
        out_shape=jax.ShapeDtypeStruct((repeats, sessions, features), bf16),
        in_specs=[anywhere] * 6,
        out_specs=pl.BlockSpec(memory_space=pltpu.VMEM),
        scratch_shapes=[
            pltpu.SMEM((sessions,), jnp.int32),
            pltpu.VMEM((sessions, features), bf16),
            pltpu.VMEM((sessions, width), bf16),
            pltpu.VMEM((sessions, width), bf16),
            pltpu.VMEM((sessions, cache_len, width), bf16),
            pltpu.VMEM((sessions, cache_len, width), bf16),
            pltpu.VMEM((columns, HEAD_SIZE), f32),
            pltpu.VMEM((columns, cache_len), bf16),
            pltpu.VMEM((columns, width), f32),
            pltpu.VMEM((columns, HEAD_SIZE), f32),
            pltpu.SemaphoreType.DMA((4,)),
            pltpu.SemaphoreType.DMA((2, sessions)),
        ],
        compiler_params=pltpu.CompilerParams(vmem_limit_bytes=14 * MIB),
        cost_estimate=pl.CostEstimate(
            flops=4 * columns * cache_len * width,
            bytes_accessed=4 * sessions * cache_len * width,
            transcendentals=columns * cache_len,
        ),
    )(*in_hbm(*args))


def base_kernel(which, p0, pa, pb, w_own, w_other, after, base_out):
    piece = p0.shape[0]
    cols = w_own.shape[1]
    rows = jnp.concatenate([p0[...], pa[...], pb[...]], axis=0)
    for i, w in enumerate((w_own, w_other)):
        at = pl.ds(pl.multiple_of(which[i] * cols, LANES), cols)
        base_out[:, at] = jnp.dot(rows, w[...], preferred_element_type=f32).astype(bf16)


def base_terms(which, pieces, w_own, w_other, after):
    count = sum(p.shape[0] for p in pieces)
    cols = w_own.shape[1]
    vmem = pl.BlockSpec(memory_space=pltpu.VMEM)
    return pl.pallas_call(
        base_kernel,
        out_shape=jax.ShapeDtypeStruct((count, 2 * cols), bf16),
        in_specs=[pl.BlockSpec(memory_space=pltpu.SMEM)]
        + [vmem] * 5
        + [pl.BlockSpec(memory_space=pl.ANY)],
        out_specs=vmem,
        compiler_params=pltpu.CompilerParams(vmem_limit_bytes=5 * MIB),
        cost_estimate=pl.CostEstimate(
            flops=4 * count * pieces[0].shape[1] * cols, bytes_accessed=2 * MIB, transcendentals=0
        ),
    )(which, *pieces, w_own, w_other, after)


def rank_kernel(
    first, which, slots, p0, pa, pb, p2, down_own, down_other, w_own, w_other, after, out, rows
):
    piece = p0.shape[0]
    for k, p in enumerate((p0, pa, pb, p2)):
        rows[k * piece : (k + 1) * piece, :] = p[...]
    kept, rank, features = down_own.shape
    cols = w_own.shape[1]
    acc = jnp.zeros((rank, slots.shape[1]), f32)
    for i, down in enumerate((down_own, down_other)):
        portion = lax.dot_general(
            down[...].reshape(kept * rank, features),
            rows[...],
            (((1,), (1,)), ((), ())),
            preferred_element_type=f32,
        )
        for j in range(kept):
            acc = acc + jnp.where(
                slots[...] == first[i] + j, portion[j * rank : (j + 1) * rank, :], 0.0
            )
    out[:rank, :] = acc.astype(bf16)
    for i, w in enumerate((w_own, w_other)):
        at = pl.ds(pl.multiple_of(which[i] * cols, LANES), cols)
        out[rank:, at] = jnp.dot(p2[...], w[...], preferred_element_type=f32).astype(bf16)


def rank_terms(first, which, slots, pieces, down_own, down_other, w_own, w_other, after):
    count = slots.shape[1]
    piece, features = pieces[0].shape
    kept, rank, features = down_own.shape
    vmem = pl.BlockSpec(memory_space=pltpu.VMEM)
    smem = pl.BlockSpec(memory_space=pltpu.SMEM)
    return pl.pallas_call(
        rank_kernel,
        out_shape=jax.ShapeDtypeStruct((rank + piece, count), bf16),
        in_specs=[smem, smem] + [vmem] * 9 + [pl.BlockSpec(memory_space=pl.ANY)],
        out_specs=vmem,
        scratch_shapes=[pltpu.VMEM((count, features), bf16)],
        compiler_params=pltpu.CompilerParams(vmem_limit_bytes=12 * MIB),
        cost_estimate=pl.CostEstimate(
            flops=4 * count * features * kept * rank, bytes_accessed=6 * MIB, transcendentals=0
        ),
    )(first, which, slots, *pieces, down_own, down_other, w_own, w_other, after)


def scaled_rows(spread, up_own, up_other, outs):
    kept_rank, quarter = up_own.shape
    piece = outs[0].shape[0]
    step = 512
    for n in range(0, quarter, step):
        cols = slice(n, n + step)
        delta = jnp.dot(
            spread[:, :kept_rank], up_own[:, cols], preferred_element_type=f32
        ) + jnp.dot(spread[:, kept_rank:], up_other[:, cols], preferred_element_type=f32)
        delta = (adapter_scale * delta.astype(bf16).astype(f32)).astype(bf16)
        for k, o in enumerate(outs):
            o[:, cols] = delta[k * piece : (k + 1) * piece, :]


def expand_last_kernel(first, slots, r0, r1, r2, r3, up_own, up_other, o2, spread, spread2):
    count = slots.shape[1]
    kept_rank = up_own.shape[0]
    piece = o2.shape[0]
    rank = r0.shape[0] - piece
    head = count - piece
    summed = (r0[...].astype(f32) + r1[...].astype(f32)) + (
        r2[...].astype(f32) + r3[...].astype(f32)
    )
    ranks = summed[:rank, :].T
    both = jnp.concatenate([ranks, ranks], axis=1)
    slot_rows = jnp.broadcast_to(slots[...].astype(f32), (LANES, count)).T
    part = lax.broadcasted_iota(jnp.int32, (1, LANES), 1) // rank
    for which in range(2):
        for j in range(kept_rank // LANES):
            slot = (first[which] + 2 * j + part).astype(f32)
            at = which * kept_rank + j * LANES
            block = jnp.where(slot_rows == slot, both, 0.0).astype(bf16)
            spread[:, at : at + LANES] = block[:head, :]
            spread2[:, at : at + LANES] = block[head:, :]
    scaled_rows(spread2, up_own, up_other, (o2,))

    @pl.when(first[3] == 1)
    def _():
        at = pl.ds(pl.multiple_of(first[2], LANES), count)
        o2[:, at] = (o2[:, at].astype(f32) + summed[rank:, :]).astype(bf16)


def expand_last(first, slots, ranks, up_own, up_other):
    count = slots.shape[1]
    kept_rank, quarter = up_own.shape
    piece = count // NY
    vmem = pl.BlockSpec(memory_space=pltpu.VMEM)
    smem = pl.BlockSpec(memory_space=pltpu.SMEM)
    return pl.pallas_call(
        expand_last_kernel,
        out_shape=(
            jax.ShapeDtypeStruct((piece, quarter), bf16),
            jax.ShapeDtypeStruct((count - piece, 2 * kept_rank), bf16),
        ),
        in_specs=[smem] + [vmem] * 7,
        out_specs=(vmem,) * 2,
        scratch_shapes=[pltpu.VMEM((piece, 2 * kept_rank), bf16)],
        compiler_params=pltpu.CompilerParams(vmem_limit_bytes=10 * MIB),
        cost_estimate=pl.CostEstimate(
            flops=4 * piece * kept_rank * quarter, bytes_accessed=4 * MIB, transcendentals=0
        ),
    )(first, slots, *ranks, up_own, up_other)


def expand_kernel(first, spread, up_own, up_other, base, *outs):
    scaled_rows(spread, up_own, up_other, outs)

    @pl.when(first[3] == 1)
    def _():
        piece = outs[0].shape[0]
        at = pl.ds(pl.multiple_of(first[2], LANES), base.shape[1])
        for k, o in enumerate(outs):
            o[:, at] = (o[:, at].astype(f32) + base[k * piece : (k + 1) * piece, :]).astype(bf16)


def expand(first, spread, up_own, up_other, base):
    quarter = up_own.shape[1]
    piece = spread.shape[0] // (NY - 1)
    vmem = pl.BlockSpec(memory_space=pltpu.VMEM)
    return pl.pallas_call(
        expand_kernel,
        out_shape=(jax.ShapeDtypeStruct((piece, quarter), bf16),) * (NY - 1),
        in_specs=[pl.BlockSpec(memory_space=pltpu.SMEM)] + [vmem] * 4,
        out_specs=(vmem,) * (NY - 1),
        compiler_params=pltpu.CompilerParams(vmem_limit_bytes=10 * MIB),
        cost_estimate=pl.CostEstimate(
            flops=2 * spread.size * quarter, bytes_accessed=5 * MIB, transcendentals=0
        ),
    )(first, spread, up_own, up_other, base)


def gather_kernel(up_own, up_other, b0, b1, b2, b3, after, own_out, other_out, base_out, sems):
    copies = [
        pltpu.make_async_copy(src, dst, sems.at[i])
        for i, (src, dst) in enumerate(((up_own, own_out), (up_other, other_out)))
    ]
    for copy in copies:
        copy.start()
    base_out[...] = (b0[...].astype(f32) + b1[...].astype(f32)) + (
        b2[...].astype(f32) + b3[...].astype(f32)
    )
    for copy in copies:
        copy.wait()


def gather_ups(up_own, up_other, parts, after):
    vmem = pl.BlockSpec(memory_space=pltpu.VMEM)
    anywhere = pl.BlockSpec(memory_space=pl.ANY)
    return pl.pallas_call(
        gather_kernel,
        out_shape=(
            jax.ShapeDtypeStruct(up_own.shape, bf16),
            jax.ShapeDtypeStruct(up_other.shape, bf16),
            jax.ShapeDtypeStruct(parts[0].shape, f32),
        ),
        in_specs=[anywhere] * 2 + [vmem] * NX + [anywhere],
        out_specs=(vmem,) * 3,
        scratch_shapes=[pltpu.SemaphoreType.DMA((2,))],
        compiler_params=pltpu.CompilerParams(vmem_limit_bytes=10 * MIB),
        cost_estimate=pl.CostEstimate(flops=MIB, bytes_accessed=8 * MIB, transcendentals=0),
    )(*in_hbm(up_own, up_other), *parts, after)


def swap_cores(x):
    return lax.ppermute(x, "c", [(0, 1), (1, 0)])


def along_y(x, way):
    pairs = []
    for y in range(NY):
        for c in range(NC):
            step = way if c == 0 else -way
            pairs.append((y * NC + c, ((y + step) % NY) * NC + c))
    return lax.ppermute(x, ("y", "c"), pairs)


def to_root(x, shift):
    pairs = []
    for z in range(NZ):
        owner = z // (NZ // NX)
        pairs.append((z * NX + (owner - shift) % NX, z * NX + owner))
    return lax.ppermute(x, ("z", "x"), pairs)


def along_x(x, shift):
    return lax.ppermute(x, "x", [(i, (i + shift) % NX) for i in range(NX)])


def local(
    query,
    incoming_key,
    incoming_value,
    cycle_key_cache,
    cycle_value_cache,
    position,
    tenant,
    tenant_adapter_index,
    output_weight,
    adapter_down_weight,
    adapter_up_weight,
):
    kept, features, rank = adapter_down_weight.shape
    cols = output_weight.shape[1]
    quarter = adapter_up_weight.shape[2]
    mine_n = query.shape[0]
    block = NZ * mine_n
    z_here, y_here, core, x_here = (lax.axis_index(a) for a in ("z", "y", "c", "x"))
    home = (z_here * NY + y_here) * NC + core
    other = home + 1 - 2 * core
    down = jnp.swapaxes(adapter_down_weight, 1, 2)
    up = adapter_up_weight.reshape(kept * rank, quarter)

    copies = attend(
        query,
        incoming_key,
        incoming_value,
        cycle_key_cache,
        cycle_value_cache,
        position,
        NZ,
    )
    down_other = swap_cores(down)
    w_other = swap_cores(output_weight)
    up_other = swap_cores(up)
    p0 = lax.all_to_all(copies, "z", 0, 0, tiled=True).reshape(block, features)

    tenants_all = tenant_adapter_index.shape[0]
    matches = tenant[:, None] == jnp.arange(tenants_all, dtype=jnp.int32)[None, :]
    slot_of = jnp.sum(jnp.where(matches, tenant_adapter_index[None, :], 0), axis=1)
    table = slot_of.reshape(NZ, NY, NC, mine_n).transpose(2, 1, 0, 3).reshape(NC * NY, block)
    ahead = 1 - 2 * core
    ys = jnp.stack([y_here, y_here - ahead, y_here + ahead, y_here + 2]) % NY
    pick = (ys + core * NY)[:, None] == jnp.arange(NC * NY, dtype=jnp.int32)[None, :]
    slots = jnp.sum(jnp.where(pick[:, :, None], table[None], 0), axis=1).reshape(1, NY * block)

    pa = along_y(p0, 1)
    pb = along_y(p0, -1)
    p2 = along_y(pa, 1)

    add = lambda *xs: functools.reduce(jnp.add, [x.astype(f32) for x in xs]).astype(bf16)
    is_root = (x_here == z_here // (NZ // NX)).astype(jnp.int32)
    width = NC * cols
    columns = (z_here % (NZ // NX)) * NY
    which = jnp.stack([core, 1 - core])
    first = jnp.stack([home * kept, other * kept, (columns + y_here) * width, is_root])

    base_part = base_terms(which, (p0, pa, pb), output_weight, w_other, down_other)
    packed = rank_terms(
        first, which, slots, (p0, pa, pb, p2), down, down_other, output_weight, w_other, base_part
    )
    packs = [packed] + [along_x(packed, s) for s in (2, 1, 3)]
    sums = [base_part] + [to_root(base_part, s) for s in (2, 1, 3)]
    *ups, base = gather_ups(up, up_other, sums, packed)
    d2, spread = expand_last(first, slots, packs, *ups)
    e2 = along_y(d2, 1)
    d0, da, db = expand(first, spread, *ups, base)

    ea = along_y(da, -1)
    eb = along_y(add(db, e2), 1)
    home_rows = add(d0, ea, eb)
    got = lax.all_to_all(home_rows.reshape(NZ, mine_n, quarter), "z", 0, 0, tiled=True)
    return jnp.sum(got.astype(f32), axis=0).astype(bf16)


def solution(mesh):
    fine = Mesh(np.asarray(mesh.devices).reshape(NZ, NY, NC, NX), DP + ("x",))
    return jax.shard_map(
        local,
        mesh=fine,
        in_specs=(
            P(DP, "x"),
            P(DP, "x"),
            P(DP, "x"),
            P(DP, None, "x"),
            P(DP, None, "x"),
            P(DP),
            P(),
            P(),
            P("x", DP),
            P(DP, "x", None),
            P(DP, None, "x"),
        ),
        out_specs=P(DP, "x"),
        check_vma=False,
    )
```

```python
import functools

import jax
import jax.numpy as jnp
import numpy as np
from jax import lax
from jax.experimental import pallas as pl
from jax.experimental.pallas import tpu as pltpu
from jax.sharding import Mesh, PartitionSpec as P

HEAD_SIZE = 128
adapter_scale = 0.5
NZ, NY, NC, NX = 8, 4, 2, 4
DP = ("z", "y", "c")
LANES = 128
MIB = 1 << 20
bf16, f32 = jnp.bfloat16, jnp.float32


def in_hbm(*xs):
    return [pltpu.with_memory_space_constraint(x, pltpu.HBM) for x in xs]


def attend_kernel(
    position, query, fresh_key, fresh_value, keys, values,
    out,
    pos, q_buf, fk_buf, fv_buf, k_buf, v_buf,
    q_rows, probs, fresh_part, o_rows, small_sems, sems,
):
    sessions, cache_len, width = keys.shape
    heads_kv = width // HEAD_SIZE
    heads = query.shape[1] // HEAD_SIZE
    group = heads // heads_kv
    small = [
        pltpu.make_async_copy(src, dst, small_sems.at[i])
        for i, (src, dst) in enumerate(
            ((query, q_buf), (position, pos), (fresh_key, fk_buf), (fresh_value, fv_buf))
        )
    ]
    key_copies = [
        pltpu.make_async_copy(keys.at[s], k_buf.at[s], sems.at[0, s]) for s in range(sessions)
    ]
    value_copies = [
        pltpu.make_async_copy(values.at[s], v_buf.at[s], sems.at[1, s]) for s in range(sessions)
    ]
    for copy in small + key_copies:
        copy.start()

    small[0].wait()
    for h in range(heads):
        q_rows[pl.ds(h, sessions, stride=heads), :] = q_buf[
            :, h * HEAD_SIZE : (h + 1) * HEAD_SIZE
        ].astype(f32)
    for copy in small[1:]:
        copy.wait()
    inverse = HEAD_SIZE ** (-0.5)
    rows_all = sessions * heads
    of_row = lax.broadcasted_iota(jnp.int32, (rows_all, 1), 0)
    kv_of_row = (of_row % heads) // group
    wide = jnp.concatenate(
        [jnp.where(kv_of_row == kv, q_rows[...], 0.0) for kv in range(heads_kv)], axis=1
    )
    wide_low = wide.astype(bf16)
    fresh_keys, fresh_values = fk_buf[...].astype(f32), fv_buf[...].astype(f32)
    fresh_key_rows = []
    fresh_value_rows = []
    for s in range(sessions):
        fresh_key_rows.append(jnp.broadcast_to(fresh_keys[s : s + 1, :], (heads, width)))
        fresh_value_rows.append(jnp.broadcast_to(fresh_values[s : s + 1, :], (heads, width)))
    fresh = (
        jnp.sum(wide * jnp.concatenate(fresh_key_rows, axis=0), axis=1, keepdims=True) * inverse
    )
    values_of_rows = jnp.concatenate(fresh_value_rows, axis=0)
    slots = lax.broadcasted_iota(jnp.int32, (1, cache_len), 1)
    batch = sessions // 2
    for g in range(0, sessions, batch):
        for s in range(g, g + batch):
            key_copies[s].wait()
            value_copies[s].start()
        for s in range(g, g + batch):
            rows = slice(s * heads, (s + 1) * heads)
            scores = lax.dot_general(
                wide_low[rows, :], k_buf[s], (((1,), (1,)), ((), ())), preferred_element_type=f32
            )
            live = (slots < pos[s]) & (slots != lax.rem(pos[s], cache_len))
            scores = jnp.where(live, scores * inverse, jnp.float32(-1e30))
            top = jnp.maximum(jnp.max(scores, axis=1, keepdims=True), fresh[rows, :])
            weights = jnp.exp(scores - top)
            fresh_weight = jnp.exp(fresh[rows, :] - top)
            scale = 1.0 / (jnp.sum(weights, axis=1, keepdims=True) + fresh_weight)
            probs[rows, :] = (weights * scale).astype(bf16)
            fresh_part[rows, :] = (fresh_weight * scale).astype(bf16).astype(
                f32
            ) * values_of_rows[rows, :]
    for g in range(0, sessions, batch):
        for s in range(g, g + batch):
            value_copies[s].wait()
        for s in range(g, g + batch):
            rows = slice(s * heads, (s + 1) * heads)
            both = (
                jnp.dot(probs[rows, :], v_buf[s], preferred_element_type=f32) + fresh_part[rows, :]
            )
            for kv in range(heads_kv):
                o_rows[s * heads + kv * group : s * heads + (kv + 1) * group, :] = both[
                    kv * group : (kv + 1) * group, kv * HEAD_SIZE : (kv + 1) * HEAD_SIZE
                ]
    for h in range(heads):
        rounded = o_rows[pl.ds(h, sessions, stride=heads), :].astype(bf16)
        for k in range(out.shape[0]):
            out[k, :, h * HEAD_SIZE : (h + 1) * HEAD_SIZE] = rounded


def attend(query, incoming_key, incoming_value, keys, values, position, repeats):
    sessions, cache_len, width = keys.shape
    features = query.shape[1]
    heads = features // HEAD_SIZE
    columns = sessions * heads
    anywhere = pl.BlockSpec(memory_space=pl.ANY)
    args = (position, query, incoming_key, incoming_value, keys, values)
    return pl.pallas_call(
        attend_kernel,
        out_shape=jax.ShapeDtypeStruct((repeats, sessions, features), bf16),
        in_specs=[anywhere] * 6,
        out_specs=pl.BlockSpec(memory_space=pltpu.VMEM),
        scratch_shapes=[
            pltpu.SMEM((sessions,), jnp.int32),
            pltpu.VMEM((sessions, features), bf16),
            pltpu.VMEM((sessions, width), bf16),
            pltpu.VMEM((sessions, width), bf16),
            pltpu.VMEM((sessions, cache_len, width), bf16),
            pltpu.VMEM((sessions, cache_len, width), bf16),
            pltpu.VMEM((columns, HEAD_SIZE), f32),
            pltpu.VMEM((columns, cache_len), bf16),
            pltpu.VMEM((columns, width), f32),
            pltpu.VMEM((columns, HEAD_SIZE), f32),
            pltpu.SemaphoreType.DMA((4,)),
            pltpu.SemaphoreType.DMA((2, sessions)),
        ],
        compiler_params=pltpu.CompilerParams(vmem_limit_bytes=14 * MIB),
        cost_estimate=pl.CostEstimate(
            flops=4 * columns * cache_len * width,
            bytes_accessed=4 * sessions * cache_len * width,
            transcendentals=columns * cache_len,
        ),
    )(*in_hbm(*args))


def base_kernel(which, p0, pa, pb, w_own, w_other, after, base_out):
    piece = p0.shape[0]
    cols = w_own.shape[1]
    rows = jnp.concatenate([p0[...], pa[...], pb[...]], axis=0)
    for i, w in enumerate((w_own, w_other)):
        at = pl.ds(pl.multiple_of(which[i] * cols, LANES), cols)
        base_out[:, at] = jnp.dot(rows, w[...], preferred_element_type=f32).astype(bf16)


def base_terms(which, pieces, w_own, w_other, after):
    count = sum(p.shape[0] for p in pieces)
    cols = w_own.shape[1]
    vmem = pl.BlockSpec(memory_space=pltpu.VMEM)
    return pl.pallas_call(
        base_kernel,
        out_shape=jax.ShapeDtypeStruct((count, 2 * cols), bf16),
        in_specs=[pl.BlockSpec(memory_space=pltpu.SMEM)]
        + [vmem] * 5
        + [pl.BlockSpec(memory_space=pl.ANY)],
        out_specs=vmem,
        compiler_params=pltpu.CompilerParams(vmem_limit_bytes=5 * MIB),
        cost_estimate=pl.CostEstimate(
            flops=4 * count * pieces[0].shape[1] * cols, bytes_accessed=2 * MIB, transcendentals=0
        ),
    )(which, *pieces, w_own, w_other, after)


def rank_kernel(
    first, which, slots, p0, pa, pb, p2, down_own, down_other, w_own, w_other, after, out, rows
):
    piece = p0.shape[0]
    for k, p in enumerate((p0, pa, pb, p2)):
        rows[k * piece : (k + 1) * piece, :] = p[...]
    kept, rank, features = down_own.shape
    cols = w_own.shape[1]
    acc = jnp.zeros((rank, slots.shape[1]), f32)
    for i, down in enumerate((down_own, down_other)):
        portion = lax.dot_general(
            down[...].reshape(kept * rank, features),
            rows[...],
            (((1,), (1,)), ((), ())),
            preferred_element_type=f32,
        )
        for j in range(kept):
            acc = acc + jnp.where(
                slots[...] == first[i] + j, portion[j * rank : (j + 1) * rank, :], 0.0
            )
    out[:rank, :] = acc.astype(bf16)
    for i, w in enumerate((w_own, w_other)):
        at = pl.ds(pl.multiple_of(which[i] * cols, LANES), cols)
        out[rank:, at] = jnp.dot(p2[...], w[...], preferred_element_type=f32).astype(bf16)


def rank_terms(first, which, slots, pieces, down_own, down_other, w_own, w_other, after):
    count = slots.shape[1]
    piece, features = pieces[0].shape
    kept, rank, features = down_own.shape
    vmem = pl.BlockSpec(memory_space=pltpu.VMEM)
    smem = pl.BlockSpec(memory_space=pltpu.SMEM)
    return pl.pallas_call(
        rank_kernel,
        out_shape=jax.ShapeDtypeStruct((rank + piece, count), bf16),
        in_specs=[smem, smem] + [vmem] * 9 + [pl.BlockSpec(memory_space=pl.ANY)],
        out_specs=vmem,
        scratch_shapes=[pltpu.VMEM((count, features), bf16)],
        compiler_params=pltpu.CompilerParams(vmem_limit_bytes=12 * MIB),
        cost_estimate=pl.CostEstimate(
            flops=4 * count * features * kept * rank, bytes_accessed=6 * MIB, transcendentals=0
        ),
    )(first, which, slots, *pieces, down_own, down_other, w_own, w_other, after)


def scaled_rows(spread, up_own, up_other, outs):
    kept_rank, quarter = up_own.shape
    piece = outs[0].shape[0]
    step = 512
    for n in range(0, quarter, step):
        cols = slice(n, n + step)
        delta = jnp.dot(
            spread[:, :kept_rank], up_own[:, cols], preferred_element_type=f32
        ) + jnp.dot(spread[:, kept_rank:], up_other[:, cols], preferred_element_type=f32)
        delta = (adapter_scale * delta.astype(bf16).astype(f32)).astype(bf16)
        for k, o in enumerate(outs):
            o[:, cols] = delta[k * piece : (k + 1) * piece, :]


def expand_kernel(
    first, slots, r0, r1, r2, r3, up_own, up_other, base, o0, oa, ob, o2, spread
):
    outs = (o0, oa, ob, o2)
    count = slots.shape[1]
    kept_rank = up_own.shape[0]
    piece = o2.shape[0]
    rank = r0.shape[0] - piece
    summed = (r0[...].astype(f32) + r1[...].astype(f32)) + (
        r2[...].astype(f32) + r3[...].astype(f32)
    )
    ranks = summed[:rank, :].T
    both = jnp.concatenate([ranks, ranks], axis=1)
    slot_rows = jnp.broadcast_to(slots[...].astype(f32), (LANES, count)).T
    part = lax.broadcasted_iota(jnp.int32, (1, LANES), 1) // rank
    for which in range(2):
        for j in range(kept_rank // LANES):
            slot = (first[which] + 2 * j + part).astype(f32)
            at = which * kept_rank + j * LANES
            spread[:, at : at + LANES] = jnp.where(slot_rows == slot, both, 0.0).astype(bf16)
    scaled_rows(spread, up_own, up_other, outs)

    @pl.when(first[3] == 1)
    def _():
        at = pl.ds(pl.multiple_of(first[2], LANES), count)
        o2[:, at] = (o2[:, at].astype(f32) + summed[rank:, :]).astype(bf16)
        for k, o in enumerate((o0, oa, ob)):
            o[:, at] = (o[:, at].astype(f32) + base[k * piece : (k + 1) * piece, :]).astype(bf16)


def expand(first, slots, ranks, up_own, up_other, base):
    count = slots.shape[1]
    kept_rank, quarter = up_own.shape
    piece = count // NY
    vmem = pl.BlockSpec(memory_space=pltpu.VMEM)
    smem = pl.BlockSpec(memory_space=pltpu.SMEM)
    return pl.pallas_call(
        expand_kernel,
        out_shape=(jax.ShapeDtypeStruct((piece, quarter), bf16),) * NY,
        in_specs=[smem] + [vmem] * 8,
        out_specs=(vmem,) * NY,
        scratch_shapes=[pltpu.VMEM((count, 2 * kept_rank), bf16)],
        compiler_params=pltpu.CompilerParams(vmem_limit_bytes=12 * MIB),
        cost_estimate=pl.CostEstimate(
            flops=4 * count * kept_rank * quarter, bytes_accessed=6 * MIB, transcendentals=0
        ),
    )(first, slots, *ranks, up_own, up_other, base)


def gather_kernel(up_own, up_other, b0, b1, b2, b3, after, own_out, other_out, base_out, sems):
    copies = [
        pltpu.make_async_copy(src, dst, sems.at[i])
        for i, (src, dst) in enumerate(((up_own, own_out), (up_other, other_out)))
    ]
    for copy in copies:
        copy.start()
    base_out[...] = (b0[...].astype(f32) + b1[...].astype(f32)) + (
        b2[...].astype(f32) + b3[...].astype(f32)
    )
    for copy in copies:
        copy.wait()


def gather_ups(up_own, up_other, parts, after):
    vmem = pl.BlockSpec(memory_space=pltpu.VMEM)
    anywhere = pl.BlockSpec(memory_space=pl.ANY)
    return pl.pallas_call(
        gather_kernel,
        out_shape=(
            jax.ShapeDtypeStruct(up_own.shape, bf16),
            jax.ShapeDtypeStruct(up_other.shape, bf16),
            jax.ShapeDtypeStruct(parts[0].shape, f32),
        ),
        in_specs=[anywhere] * 2 + [vmem] * NX + [anywhere],
        out_specs=(vmem,) * 3,
        scratch_shapes=[pltpu.SemaphoreType.DMA((2,))],
        compiler_params=pltpu.CompilerParams(vmem_limit_bytes=10 * MIB),
        cost_estimate=pl.CostEstimate(flops=MIB, bytes_accessed=8 * MIB, transcendentals=0),
    )(*in_hbm(up_own, up_other), *parts, after)


def swap_cores(x):
    return lax.ppermute(x, "c", [(0, 1), (1, 0)])


def along_y(x, way):
    pairs = []
    for y in range(NY):
        for c in range(NC):
            step = way if c == 0 else -way
            pairs.append((y * NC + c, ((y + step) % NY) * NC + c))
    return lax.ppermute(x, ("y", "c"), pairs)


def to_root(x, shift):
    pairs = []
    for z in range(NZ):
        owner = z // (NZ // NX)
        pairs.append((z * NX + (owner - shift) % NX, z * NX + owner))
    return lax.ppermute(x, ("z", "x"), pairs)


def along_x(x, shift):
    return lax.ppermute(x, "x", [(i, (i + shift) % NX) for i in range(NX)])


def local(
    query,
    incoming_key,
    incoming_value,
    cycle_key_cache,
    cycle_value_cache,
    position,
    tenant,
    tenant_adapter_index,
    output_weight,
    adapter_down_weight,
    adapter_up_weight,
):
    kept, features, rank = adapter_down_weight.shape
    cols = output_weight.shape[1]
    quarter = adapter_up_weight.shape[2]
    mine_n = query.shape[0]
    block = NZ * mine_n
    z_here, y_here, core, x_here = (lax.axis_index(a) for a in ("z", "y", "c", "x"))
    home = (z_here * NY + y_here) * NC + core
    other = home + 1 - 2 * core
    down = jnp.swapaxes(adapter_down_weight, 1, 2)
    up = adapter_up_weight.reshape(kept * rank, quarter)

    copies = attend(
        query,
        incoming_key,
        incoming_value,
        cycle_key_cache,
        cycle_value_cache,
        position,
        NZ,
    )
    down_other = swap_cores(down)
    w_other = swap_cores(output_weight)
    up_other = swap_cores(up)
    p0 = lax.all_to_all(copies, "z", 0, 0, tiled=True).reshape(block, features)

    tenants_all = tenant_adapter_index.shape[0]
    matches = tenant[:, None] == jnp.arange(tenants_all, dtype=jnp.int32)[None, :]
    slot_of = jnp.sum(jnp.where(matches, tenant_adapter_index[None, :], 0), axis=1)
    table = slot_of.reshape(NZ, NY, NC, mine_n).transpose(2, 1, 0, 3).reshape(NC * NY, block)
    ahead = 1 - 2 * core
    ys = jnp.stack([y_here, y_here - ahead, y_here + ahead, y_here + 2]) % NY
    pick = (ys + core * NY)[:, None] == jnp.arange(NC * NY, dtype=jnp.int32)[None, :]
    slots = jnp.sum(jnp.where(pick[:, :, None], table[None], 0), axis=1).reshape(1, NY * block)

    pa = along_y(p0, 1)
    pb = along_y(p0, -1)
    p2 = along_y(pa, 1)

    add = lambda *xs: functools.reduce(jnp.add, [x.astype(f32) for x in xs]).astype(bf16)
    is_root = (x_here == z_here // (NZ // NX)).astype(jnp.int32)
    width = NC * cols
    columns = (z_here % (NZ // NX)) * NY
    which = jnp.stack([core, 1 - core])
    first = jnp.stack([home * kept, other * kept, (columns + y_here) * width, is_root])

    base_part = base_terms(which, (p0, pa, pb), output_weight, w_other, down_other)
    packed = rank_terms(
        first, which, slots, (p0, pa, pb, p2), down, down_other, output_weight, w_other, base_part
    )
    packs = [packed] + [along_x(packed, s) for s in (2, 1, 3)]
    sums = [base_part] + [to_root(base_part, s) for s in (2, 1, 3)]
    *ups, base = gather_ups(up, up_other, sums, packed)
    d0, da, db, d2 = expand(first, slots, packs, *ups, base)
    e2 = along_y(d2, 1)

    ea = along_y(da, -1)
    eb = along_y(add(db, e2), 1)
    home_rows = add(d0, ea, eb)
    got = lax.all_to_all(home_rows.reshape(NZ, mine_n, quarter), "z", 0, 0, tiled=True)
    return jnp.sum(got.astype(f32), axis=0).astype(bf16)


def solution(mesh):
    fine = Mesh(np.asarray(mesh.devices).reshape(NZ, NY, NC, NX), DP + ("x",))
    return jax.shard_map(
        local,
        mesh=fine,
        in_specs=(
            P(DP, "x"),
            P(DP, "x"),
            P(DP, "x"),
            P(DP, None, "x"),
            P(DP, None, "x"),
            P(DP),
            P(),
            P(),
            P("x", DP),
            P(DP, "x", None),
            P(DP, None, "x"),
        ),
        out_specs=P(DP, "x"),
        check_vma=False,
    )
```
